32 devices in a mesh: grp: 2 (over y), kvp: 4 (over z), tp: 4 (over x, core).
Axes of the slice: x: 2, y: 2, z: 4, core: 2. Of those that a mesh axis runs over, the one named last changes fastest.
Arguments:
- queries: bfloat16 [32, 4096], P('grp', 'tp'), parts along dimension 0, may hold values from -6 to 6
- keys: bfloat16 [32, 512, 512], P('grp', 'kvp', 'tp'), parts along dimension 0, may hold values from -6 to 6
- values: bfloat16 [32, 512, 512], P('grp', 'kvp', 'tp'), parts along dimension 0, may hold values from -6 to 6
- lengths: int32 [32], P('grp'), parts along dimension 0, may hold values from 256 to 512, as said below
- out_weight: bfloat16 [4096, 1536], P('tp', 'kvp'), may hold values from -0.375 to 0.375
- residual: bfloat16 [32, 1536], P('grp', 'kvp'), parts along dimension 0, may hold values from -20 to 20
- norm_gain: bfloat16 [1536], P('kvp'), may hold values from 0.099609375 to 1.8984375
- expert_ids: int32 [32, 4], P('grp'), parts along dimension 0, may hold values from 0 to 3, as said below
- gate_probs: float32 [32, 4], P('grp'), parts along dimension 0, may hold values from 0.2 to 1
- w_gate: bfloat16 [4, 1536, 1536], P('kvp', None, 'tp'), may hold values from -0.15625 to 0.15625
- w_up: bfloat16 [4, 1536, 1536], P('kvp', None, 'tp'), may hold values from -0.15625 to 0.15625
- w_down: bfloat16 [4, 1536, 1536], P('kvp', 'tp'), may hold values from -0.15625 to 0.15625
Outputs:
- attended: float32 [32, 4096], P('grp', 'tp'), parts along dimension 0
- mixed: bfloat16 [32, 1536], P('grp', 'kvp'), parts along dimension 0
The draws below stay inside these ranges and needn't reach their ends.
There are 2 independent parts, one for each index of `grp`. The reference program is written for one: setup_inputs(seed, part) draws one part's arguments, and reference() takes and returns one part's arrays. A program takes and returns all parts, laid end to end along the dimension named above; an argument that names none is the same for every part. Nothing has to cross between parts.
Inputs may be any that keep to these rules, and one draw needn't show every extreme that they name: `lengths`: at least one sequence has all 512 positions valid. `expert_ids`: each row names 4 different experts; no expert is named by more than 16 rows, and some expert by exactly 16.
All inputs are finite; a program needn't handle non-finite values.
Results may differ from the reference program's by a relative error of at most 0.006.
Values may be sent and summed in bfloat16 or wider, within the bound.
A program may use at most 64 MiB of HBM per device.

```python
import math
import jax
import jax.numpy as jnp
from jax import lax

D = 1536
FF = 1536
HEADS = 64
KV_HEADS = 8
HEAD = 64
TOP = 4
EXP_DEV = 1
BATCH = 16
CTX_DEV = 128
EXPERTS = 4
CONTEXT = 512
CAP = 16
N_KVP = 4


def draw_queries(key, part):
    base_draw = jnp.clip(jax.random.normal(jax.random.fold_in(key, 42), (BATCH, HEADS * HEAD), jnp.float32), -4.5, 4.5)
    return base_draw.astype(jnp.bfloat16)


def draw_keys(key, part):
    context = CTX_DEV * N_KVP
    base_draw = jnp.clip(jax.random.normal(jax.random.fold_in(key, 44), (BATCH, context, KV_HEADS * HEAD), jnp.float32), -4.5, 4.5)
    return base_draw.astype(jnp.bfloat16)


def draw_lengths(key, part):
    context = CTX_DEV * N_KVP
    drawn_len = jax.random.randint(jax.random.fold_in(key, 11), (BATCH,), 2 * CTX_DEV, context + 1)
    full_row = jax.random.randint(jax.random.fold_in(key, 12), (), 0, BATCH)
    return jnp.where(jnp.arange(BATCH) == full_row, context, drawn_len).astype(jnp.int32)


def draw_expert_ids(key, part):
    experts = EXP_DEV * N_KVP
    least_group = min(CAP, (BATCH * TOP + experts - 1) // experts)
    sizes_drawn = jax.random.randint(jax.random.fold_in(key, 21), (TOP,), least_group, CAP + 1)
    sizes_drawn = sizes_drawn.at[0].set(CAP)
    span_size = (BATCH + sizes_drawn - 1) // sizes_drawn
    offsets = jnp.cumsum(span_size) - span_size
    row_keys = jax.random.split(jax.random.fold_in(key, 22), TOP)

    def shuffle(subkey):
        return jax.random.permutation(subkey, BATCH)
    orders = jax.vmap(shuffle)(row_keys)
    slot_ids = offsets[:, None] + orders // sizes_drawn[:, None]
    labels = jax.random.permutation(jax.random.fold_in(key, 23), experts)
    return labels[slot_ids].T.astype(jnp.int32)


def draw_residual(key, part):
    rising = jnp.exp(jnp.linspace(math.log(0.5), math.log(1.5), D))
    columns = rising * jnp.exp(jax.random.uniform(jax.random.fold_in(key, 51), (D,), jnp.float32, math.log(0.6), math.log(2.0)))
    row_scale = jnp.exp(jax.random.uniform(jax.random.fold_in(key, 55), (BATCH, 1), jnp.float32, math.log(0.5), math.log(2.0)))
    base_draw = jnp.clip(jax.random.normal(jax.random.fold_in(key, 56), (BATCH, D), jnp.float32), -3.0, 3.0)
    return (base_draw * row_scale * columns[None, :]).astype(jnp.bfloat16)


def shard_levels(own_key, shape, cuts, smallest, largest):
    gain = 1.0
    for dim, parts in cuts:
        draws = jax.random.uniform(jax.random.fold_in(jax.random.fold_in(own_key, 6), dim), (parts,), jnp.float32, smallest / len(cuts), largest / len(cuts))
        gain = gain * jnp.repeat(jnp.exp(draws), shape[dim] // parts).reshape((-1,) + (1,) * (len(shape) - 1 - dim))
    return gain


def centred(stream_key, extent, scale, bound, cuts=(), kind=jnp.bfloat16):
    entries = scale * jax.random.normal(stream_key, extent, jnp.float32)
    if cuts:
        entries = entries * shard_levels(stream_key, extent, cuts, -0.22, 0.18)
    return jnp.clip(entries, -bound, bound).astype(kind)


def setup_inputs(seed: int = 0, part: int = 0) -> dict:
    streams_of = jax.random.split(jax.random.key(seed), 13)
    part_splits = jax.random.split(jax.random.fold_in(streams_of[12], part), 13)
    queries = draw_queries(jax.random.fold_in(jax.random.fold_in(streams_of[12], part), 71), part)
    keys = draw_keys(jax.random.fold_in(jax.random.fold_in(streams_of[12], part), 71), part)
    values = centred(part_splits[2], (BATCH, CONTEXT, KV_HEADS * HEAD), 1.0, 6.0, ((1, 4), (2, 4)))
    lengths = draw_lengths(jax.random.fold_in(jax.random.fold_in(streams_of[12], part), 71), part)
    out_weight = centred(streams_of[4], (HEADS * HEAD, D), (4 * HEAD) ** -0.5, 0.375, ((0, 4), (1, 4)))
    residual = draw_residual(jax.random.fold_in(jax.random.fold_in(streams_of[12], part), 71), part)
    norm_gain = jnp.clip(1.0 + 0.18 * jax.random.normal(streams_of[6], (D,), jnp.float32), 0.099609375, 1.8984375).astype(jnp.bfloat16)
    expert_ids = draw_expert_ids(jax.random.fold_in(jax.random.fold_in(streams_of[12], part), 71), part)
    gate_probs = jnp.clip(jax.random.uniform(part_splits[8], (BATCH, TOP), jnp.float32, 0.2, 1.0), 0.2, 1.0)
    w_gate = centred(streams_of[9], (EXPERTS, D, FF), D ** -0.5, 0.15625, ((0, 4), (2, 4)))
    w_up = centred(streams_of[10], (EXPERTS, D, FF), D ** -0.5, 0.15625, ((0, 4), (2, 4)))
    w_down = centred(streams_of[11], (EXPERTS, FF, D), FF ** -0.5, 0.15625, ((0, 4), (1, 4)))
    return {"queries": queries, "keys": keys, "values": values, "lengths": lengths, "out_weight": out_weight, "residual": residual, "norm_gain": norm_gain, "expert_ids": expert_ids, "gate_probs": gate_probs, "w_gate": w_gate, "w_up": w_up, "w_down": w_down}


EPSILON = 1e-05
NEGATIVE = -1e+30

def slot_tables(expert_ids, gate_probs, experts, capacity):
    batch_size, top_count = expert_ids.shape
    flat_ids = expert_ids.reshape(-1)
    pair_count = flat_ids.shape[0]
    pair_order = jnp.arange(pair_count, dtype=jnp.int32)
    earlier_same = (flat_ids[:, None] == flat_ids[None, :]) & (pair_order[None, :] < pair_order[:, None])
    slot_index = lax.optimization_barrier(jnp.sum(earlier_same.astype(jnp.int32), axis=1))
    target_col = flat_ids * capacity + slot_index
    columns = jnp.arange(experts * capacity, dtype=jnp.int32)
    hit_table = (target_col[:, None] == columns[None, :]).astype(jnp.float32)
    hit_table = hit_table.reshape(batch_size, top_count, experts * capacity)
    dispatch = lax.optimization_barrier(jnp.sum(hit_table, axis=1))
    combine = lax.optimization_barrier(jnp.sum(hit_table * gate_probs[:, :, None], axis=1))
    return (dispatch, combine)

def run_expert(operands):
    expert_rows, gate_w, up_w, down_w = operands
    gate_proj = jnp.dot(expert_rows, gate_w, preferred_element_type=jnp.float32)
    up_proj = jnp.dot(expert_rows, up_w, preferred_element_type=jnp.float32)
    activation = (jax.nn.silu(gate_proj) * up_proj).astype(jnp.bfloat16)
    return jnp.dot(activation, down_w, preferred_element_type=jnp.float32)

def reference(queries, keys, values, lengths, out_weight, residual, norm_gain, expert_ids, gate_probs, w_gate, w_up, w_down):
    batch_size = queries.shape[0]
    group_size = HEADS // KV_HEADS
    query_heads = queries.astype(jnp.float32).reshape(batch_size, KV_HEADS, group_size, HEAD)
    key_blocks = keys.astype(jnp.float32).reshape(batch_size, N_KVP, CTX_DEV, KV_HEADS, HEAD)
    value_blocks = values.astype(jnp.float32).reshape(batch_size, N_KVP, CTX_DEV, KV_HEADS, HEAD)
    scores = jnp.einsum('bgrd,bncgd->bgrnc', query_heads, key_blocks) * HEAD ** (-0.5)
    position = jnp.arange(N_KVP * CTX_DEV, dtype=jnp.int32).reshape(N_KVP, CTX_DEV)
    valid_key = (position[None] < lengths[:, None, None])[:, None, None]
    masked = jnp.where(valid_key, scores, NEGATIVE)
    block_max = lax.optimization_barrier(jnp.max(masked, axis=4))
    weights = jnp.where(valid_key, jnp.exp(masked - block_max[..., None]), 0.0)
    rounded = lax.optimization_barrier(weights.astype(jnp.bfloat16)).astype(jnp.float32)
    block_sum = lax.optimization_barrier(jnp.sum(rounded, axis=4))
    block_out = jnp.einsum('bgrnc,bncgd->bgrnd', rounded, value_blocks)
    global_max = lax.optimization_barrier(jnp.max(block_max, axis=3))
    rescale = jnp.exp(block_max - global_max[..., None])
    denominator = lax.optimization_barrier(jnp.sum(rescale * block_sum, axis=3))
    attended = lax.optimization_barrier(jnp.sum(rescale[..., None] * block_out, axis=3)) / denominator[..., None]
    attended = attended.reshape(batch_size, HEADS * HEAD)
    projected = jnp.dot(attended.astype(jnp.bfloat16), out_weight, preferred_element_type=jnp.float32)
    hidden_state = lax.optimization_barrier((projected + residual.astype(jnp.float32)).astype(jnp.bfloat16))
    state_wide = hidden_state.astype(jnp.float32)
    mean_square = lax.optimization_barrier(jnp.sum(state_wide * state_wide, axis=1)) / D
    normed = (state_wide * lax.rsqrt(mean_square + EPSILON)[:, None] * norm_gain.astype(jnp.float32)[None, :]).astype(jnp.bfloat16)
    dispatch, combine = slot_tables(expert_ids, gate_probs, EXPERTS, CAP)
    expert_rows = jnp.dot(dispatch.T.astype(jnp.bfloat16), normed, preferred_element_type=jnp.float32).astype(jnp.bfloat16)
    expert_rows = expert_rows.reshape(EXPERTS, CAP, D)
    expert_out = lax.map(run_expert, (expert_rows, w_gate, w_up, w_down))
    moe_term = jnp.dot(combine, expert_out.reshape(EXPERTS * CAP, D), precision=lax.Precision.HIGHEST)
    mixed = (state_wide + moe_term).astype(jnp.bfloat16)
    return (attended, mixed)
```

```python
import jax
import jax.numpy as jnp
from jax import lax
from jax.experimental import pallas as pl
from jax.experimental.pallas import tpu as pltpu
from jax.sharding import PartitionSpec as P

MESH = pl.DeviceIdType.MESH

D = 1536
HEAD = 64


EPSILON = 1e-05
NEGATIVE = -1e30


def merged(part, axis, combine):
    gathered = jax.tree.map(lambda a: lax.all_gather(a, axis), part)

    def take(source):
        return jax.tree.map(lambda a: lax.dynamic_index_in_dim(a, source, 0, False), gathered)

    return lax.fori_loop(
        1, lax.axis_size(axis), lambda source, state: combine(state, take(source)), take(0)
    )


def slot_tables(expert_ids, gate_probs, experts, capacity):
    batch_size, top_count = expert_ids.shape
    flat_ids = expert_ids.reshape(-1)
    pair_count = flat_ids.shape[0]
    pair_order = jnp.arange(pair_count, dtype=jnp.int32)
    earlier_same = (flat_ids[:, None] == flat_ids[None, :]) & (
        pair_order[None, :] < pair_order[:, None]
    )
    slot_index = jnp.sum(earlier_same.astype(jnp.int32), axis=1)
    target_col = flat_ids * capacity + slot_index
    columns = jnp.arange(experts * capacity, dtype=jnp.int32)
    hit_table = (target_col[:, None] == columns[None, :]).astype(jnp.float32)
    hit_table = hit_table.reshape(batch_size, top_count, experts * capacity)
    dispatch = jnp.sum(hit_table, axis=1)
    combine = jnp.sum(hit_table * gate_probs[:, :, None], axis=1)
    return (dispatch, combine)


def merge_partial(earlier, latest):
    global_max = jnp.maximum(earlier[0], latest[0])
    lead_scale = jnp.exp(earlier[0] - global_max)
    trail_scale = jnp.exp(latest[0] - global_max)
    return (
        global_max,
        lead_scale * earlier[1] + trail_scale * latest[1],
        lead_scale[..., None] * earlier[2] + trail_scale[..., None] * latest[2],
    )


def on_device(
    queries,
    keys,
    values,
    lengths,
    out_weight,
    residual,
    norm_gain,
    expert_ids,
    gate_probs,
    w_gate,
    w_up,
    w_down,
):
    batch_size = queries.shape[0]
    local_kv = keys.shape[2] // HEAD
    local_heads = queries.shape[1] // HEAD
    group_size = local_heads // local_kv
    ctx_dev = keys.shape[1]
    shards = lax.axis_size("kvp")
    query_heads = queries.reshape(batch_size, local_kv, group_size, HEAD)
    key_rows = keys.reshape(batch_size, ctx_dev, local_kv, HEAD)
    value_rows = values.reshape(batch_size, ctx_dev, local_kv, HEAD)
    scores = jnp.einsum(
        "bgrd,bcgd->bgrc", query_heads, key_rows, preferred_element_type=jnp.float32
    ) * HEAD ** (-0.5)
    position = lax.axis_index("kvp") * ctx_dev + jnp.arange(ctx_dev, dtype=jnp.int32)
    valid_key = (position[None, :] < lengths[:, None])[:, None, None, :]
    masked = jnp.where(valid_key, scores, NEGATIVE)
    block_max = jnp.max(masked, axis=3)
    weights = jnp.where(valid_key, jnp.exp(masked - block_max[..., None]), 0.0)
    rounded = weights.astype(jnp.bfloat16)
    block_sum = jnp.sum(rounded.astype(jnp.float32), axis=3)
    block_out = jnp.einsum(
        "bgrc,bcgd->bgrd", rounded, value_rows, preferred_element_type=jnp.float32
    )
    global_max, denominator, summed = merged(
        (block_max, block_sum, block_out), "kvp", merge_partial
    )
    attended = (summed / denominator[..., None]).reshape(batch_size, local_heads * HEAD)
    projected = lax.psum(
        jnp.dot(attended.astype(jnp.bfloat16), out_weight, preferred_element_type=jnp.float32), "tp"
    )
    hidden_state = lax.optimization_barrier(
        (projected + residual.astype(jnp.float32)).astype(jnp.bfloat16)
    )
    state_wide = hidden_state.astype(jnp.float32)
    col_count = hidden_state.shape[1]
    exp_dev = w_gate.shape[0]
    experts = exp_dev * shards
    capacity = min(batch_size, max(2, 2 * batch_size * expert_ids.shape[1] // experts))
    dispatch, combine = slot_tables(expert_ids, gate_probs, experts, capacity)
    total_sq = lax.psum(jnp.sum(state_wide * state_wide, axis=1), "kvp")
    inverse = lax.rsqrt(total_sq / D + EPSILON)
    normed = (state_wide * inverse[:, None] * norm_gain.astype(jnp.float32)[None, :]).astype(
        jnp.bfloat16
    )
    outgoing = jnp.dot(
        dispatch.T.astype(jnp.bfloat16), normed, preferred_element_type=jnp.float32
    ).astype(jnp.bfloat16)
    outgoing = outgoing.reshape(experts, capacity, col_count)
    expert_rows = lax.all_to_all(outgoing, "kvp", split_axis=0, concat_axis=2, tiled=True)
    gate_proj = jnp.einsum("ecd,edf->ecf", expert_rows, w_gate, preferred_element_type=jnp.float32)
    up_proj = jnp.einsum("ecd,edf->ecf", expert_rows, w_up, preferred_element_type=jnp.float32)
    activation = (jax.nn.silu(gate_proj) * up_proj).astype(jnp.bfloat16)
    partial_value = jnp.einsum(
        "ecf,efd->ecd", activation, w_down, preferred_element_type=jnp.float32
    )
    returned = lax.all_to_all(partial_value, "kvp", split_axis=2, concat_axis=0, tiled=True)
    moe_local = jnp.dot(
        combine, returned.reshape(experts * capacity, col_count), precision=lax.Precision.HIGHEST
    )
    moe_term = lax.psum(moe_local, "tp")
    mixed = (state_wide + moe_term).astype(jnp.bfloat16)
    return (attended, mixed)


NORM_WIDTH = D


def peers(axis):
    count = lax.axis_size(axis)
    me = lax.axis_index(axis)
    return [(step - 1, lax.rem(me + step, count)) for step in range(1, count)]


def fused(
    q_hbm, k_hbm, v_hbm, len_ref, wo_hbm, res_ref, gain_ref, ids_ref, gp_ref, wg_hbm, wu_hbm, wd_hbm,
    att_ref, mix_ref,
    q_vm, k_vm, v_vm, wo_vm, wg_vm, wu_vm, wd_vm,
    q_rows, s_rows, o_rows, t_rows,
    o_all, stat_all, gain_all, p_all, h_all, y_send, y_recv, z_all,
    load_sem, o_send, o_recv, st_send, st_recv, g_send, g_recv,
    p_send, p_recv, h_send, h_recv, ys_send, ys_recv, z_send, z_recv,
):
    shards = o_all.shape[0]
    tps = p_all.shape[0]
    batch, width = q_vm.shape
    heads = width // HEAD
    ctx = k_vm.shape[1]
    lanes = k_vm.shape[2]
    cols = wo_vm.shape[1]
    group = heads * HEAD // lanes
    mine = lax.axis_index("kvp")
    my_tp = lax.axis_index("tp")
    kvp_peers = peers("kvp")
    tp_peers = peers("tp")

    loads = []
    for index, (source, target) in enumerate(
        ((q_hbm, q_vm), (k_hbm, k_vm), (v_hbm, v_vm), (wo_hbm, wo_vm), (wg_hbm, wg_vm), (wu_hbm, wu_vm), (wd_hbm, wd_vm))
    ):
        copy = pltpu.make_async_copy(source, target, load_sem.at[index])
        copy.start()
        loads.append(copy)
    q_load, k_load, v_load, wo_load, wg_load, wu_load, wd_load = loads

    barrier = pltpu.get_barrier_semaphore()
    for _, peer in kvp_peers:
        pl.semaphore_signal(barrier, inc=1, device_id={"kvp": peer}, device_id_type=MESH)
    for _, peer in tp_peers:
        pl.semaphore_signal(barrier, inc=1, device_id={"tp": peer}, device_id_type=MESH)

    sent = []

    def push(source, target, send, recv, place):
        copy = pltpu.make_async_remote_copy(
            src_ref=source, dst_ref=target, send_sem=send, recv_sem=recv,
            device_id=place, device_id_type=MESH,
        )
        copy.start()
        sent.append(copy)
        return copy

    lane = lax.broadcasted_iota(jnp.int32, (batch, lanes), 1)
    low = lane < HEAD
    gain_all[mine] = jnp.broadcast_to(gain_ref[...].astype(jnp.float32).reshape(1, cols), (8, cols))

    q_load.wait()
    for head in range(heads):
        pair = head // 2
        wide = q_vm[:, pair * lanes : (pair + 1) * lanes].astype(jnp.float32)
        kept = jnp.where(low if head % 2 == 0 else ~low, wide, 0.0)
        if head % 2 != head // group:
            kept = pltpu.roll(kept, HEAD, 1)
        q_rows[pl.ds(head, batch, stride=heads), :] = kept

    k_load.wait()
    position = mine * ctx + lax.broadcasted_iota(jnp.int32, (heads, ctx), 1)
    for b in range(batch):
        rows = pl.ds(b * heads, heads)
        scores = lax.dot_general(
            q_rows[rows, :].astype(jnp.bfloat16), k_vm[b],
            (((1,), (1,)), ((), ())), preferred_element_type=jnp.float32,
        ) * HEAD ** (-0.5)
        s_rows[rows, :] = jnp.where(position < len_ref[b], scores, NEGATIVE)
    v_load.wait()
    stat_low = lax.broadcasted_iota(jnp.int32, (heads, lanes), 1) < HEAD
    for b in range(batch):
        rows = pl.ds(b * heads, heads)
        masked = s_rows[rows, :]
        block_max = jnp.max(masked, axis=1, keepdims=True)
        weights = jnp.where(position < len_ref[b], jnp.exp(masked - block_max), 0.0)
        rounded = weights.astype(jnp.bfloat16)
        block_sum = jnp.sum(rounded.astype(jnp.float32), axis=1, keepdims=True)
        out = jnp.dot(rounded, v_vm[b], preferred_element_type=jnp.float32)
        o_rows[pl.ds(b, heads, stride=batch), :] = out
        t_rows[pl.ds(b, heads, stride=batch), :] = jnp.where(stat_low, block_max, block_sum)
    stat = jnp.ones((batch, lanes), jnp.float32)
    for pair in range(heads // 2):
        first = o_rows[2 * pair * batch : (2 * pair + 1) * batch, :]
        second = o_rows[(2 * pair + 1) * batch : (2 * pair + 2) * batch, :]
        if 2 * pair // group == 0:
            second = pltpu.roll(second, HEAD, 1)
        else:
            first = pltpu.roll(first, HEAD, 1)
        o_all[mine, :, pair * lanes : (pair + 1) * lanes] = jnp.where(low, first, second).astype(jnp.bfloat16)
    for head in range(heads):
        stat = jnp.where((lane == head) | (lane == HEAD + head), t_rows[head * batch : (head + 1) * batch, :], stat)
    stat_all[mine] = stat

    pl.semaphore_wait(barrier, len(kvp_peers) + len(tp_peers))
    o_copies = []
    for slot, peer in kvp_peers:
        o_copies.append(push(stat_all.at[mine], stat_all.at[mine], st_send.at[slot], st_recv.at[slot], {"kvp": peer}))
        o_copies.append(push(o_all.at[mine], o_all.at[mine], o_send.at[slot], o_recv.at[slot], {"kvp": peer}))
    g_copies = [
        push(gain_all.at[mine], gain_all.at[mine], g_send.at[slot], g_recv.at[slot], {"kvp": peer})
        for slot, peer in kvp_peers
    ]
    wo_load.wait()
    for copy in o_copies:
        copy.wait_recv()

    global_max = stat_all[0]
    for s in range(1, shards):
        global_max = jnp.maximum(global_max, stat_all[s])
    scales = []
    denominator = None
    for s in range(shards):
        stat = stat_all[s]
        scale = jnp.exp(stat - global_max)
        scales.append(scale)
        term = scale * pltpu.roll(stat, HEAD, 1)
        denominator = term if denominator is None else denominator + term
    inverse = 1.0 / denominator
    factors = [scale * inverse for scale in scales]
    parts = []
    for pair in range(heads // 2):
        block = slice(pair * lanes, (pair + 1) * lanes)
        total = None
        for s in range(shards):
            spread = jnp.where(
                low,
                jnp.broadcast_to(factors[s][:, 2 * pair : 2 * pair + 1], (batch, lanes)),
                jnp.broadcast_to(factors[s][:, 2 * pair + 1 : 2 * pair + 2], (batch, lanes)),
            )
            term = spread * o_all[s, :, block].astype(jnp.float32)
            total = term if total is None else total + term
        att_ref[:, block] = total
        parts.append(total.astype(jnp.bfloat16))
    attended = jnp.concatenate(parts, axis=1)

    p_all[my_tp] = jnp.dot(attended, wo_vm[...], preferred_element_type=jnp.float32)
    p_copies = [
        push(p_all.at[my_tp], p_all.at[my_tp], p_send.at[slot], p_recv.at[slot], {"tp": peer})
        for slot, peer in tp_peers
    ]
    gate_row = jnp.sum(jnp.where(ids_ref[...] == mine, gp_ref[...], 0.0), axis=0, keepdims=True)
    square = (batch, batch)
    diagonal = lax.broadcasted_iota(jnp.int32, square, 0) == lax.broadcasted_iota(jnp.int32, square, 1)
    expert_gate = jnp.sum(jnp.where(diagonal, jnp.broadcast_to(gate_row, square), 0.0), axis=1, keepdims=True)
    for copy in p_copies:
        copy.wait_recv()
    projected = p_all[0]
    for s in range(1, tps):
        projected = projected + p_all[s]
    hidden = (projected + res_ref[...].astype(jnp.float32)).astype(jnp.bfloat16)
    h_all[mine] = hidden
    h_copies = [
        push(h_all.at[mine], h_all.at[mine], h_send.at[slot], h_recv.at[slot], {"kvp": peer})
        for slot, peer in kvp_peers
    ]
    wg_load.wait()
    wu_load.wait()
    wd_load.wait()
    for copy in g_copies:
        copy.wait_recv()
    for copy in h_copies:
        copy.wait_recv()

    states = [h_all[s].astype(jnp.float32) for s in range(shards)]
    squares = None
    for state in states:
        term = state * state
        squares = term if squares is None else squares + term
    root = lax.rsqrt(jnp.sum(squares, axis=1, keepdims=True) / NORM_WIDTH + EPSILON)
    normed = jnp.concatenate(
        [(states[s] * root * gain_all[s, 0:1, :]).astype(jnp.bfloat16) for s in range(shards)], axis=1
    )
    gate_proj = jnp.dot(normed, wg_vm[0], preferred_element_type=jnp.float32)
    up_proj = jnp.dot(normed, wu_vm[0], preferred_element_type=jnp.float32)
    activation = (gate_proj / (1.0 + jnp.exp(-gate_proj)) * up_proj).astype(jnp.bfloat16)
    expert_out = jnp.dot(activation, wd_vm[0], preferred_element_type=jnp.float32) * expert_gate
    for s in range(shards):
        y_send[s] = expert_out[:, s * cols : (s + 1) * cols].astype(y_send.dtype)
    y_copies = [
        push(y_send.at[peer], y_recv.at[mine], ys_send.at[slot], ys_recv.at[slot], {"kvp": peer})
        for slot, peer in kvp_peers
    ]
    y_recv[mine] = y_send[mine]
    for copy in y_copies:
        copy.wait_recv()
    term = y_recv[0].astype(jnp.float32)
    for s in range(1, shards):
        term = term + y_recv[s].astype(jnp.float32)
    z_all[my_tp] = term.astype(z_all.dtype)
    z_copies = [
        push(z_all.at[my_tp], z_all.at[my_tp], z_send.at[slot], z_recv.at[slot], {"tp": peer})
        for slot, peer in tp_peers
    ]
    for copy in z_copies:
        copy.wait_recv()
    moe = z_all[0].astype(jnp.float32)
    for s in range(1, tps):
        moe = moe + z_all[s].astype(jnp.float32)
    mix_ref[...] = (hidden.astype(jnp.float32) + moe).astype(jnp.bfloat16)
    for copy in sent:
        copy.wait_send()


def on_device_fused(
    queries, keys, values, lengths, out_weight, residual, norm_gain, expert_ids, gate_probs, w_gate, w_up, w_down
):
    shards = lax.axis_size("kvp")
    tps = lax.axis_size("tp")
    batch, width = queries.shape
    heads = width // HEAD
    ctx, lanes = keys.shape[1:]
    cols = residual.shape[1]
    vmem = pl.BlockSpec(memory_space=pltpu.VMEM)
    anywhere = pl.BlockSpec(memory_space=pltpu.HBM)
    smem = pl.BlockSpec(memory_space=pltpu.SMEM)
    f32, b16 = jnp.float32, jnp.bfloat16

    def sems(count):
        return pltpu.SemaphoreType.DMA((max(count, 1),))

    k, t = shards - 1, tps - 1
    return tuple(pl.pallas_call(
        fused,
        out_shape=(
            jax.ShapeDtypeStruct((batch, width), f32),
            jax.ShapeDtypeStruct((batch, cols), b16),
        ),
        in_specs=[anywhere, anywhere, anywhere, smem, anywhere, vmem, vmem, vmem, vmem, anywhere, anywhere, anywhere],
        out_specs=(vmem, vmem),
        scratch_shapes=[
            pltpu.VMEM(queries.shape, b16),
            pltpu.VMEM(keys.shape, b16),
            pltpu.VMEM(values.shape, b16),
            pltpu.VMEM(out_weight.shape, b16),
            pltpu.VMEM(w_gate.shape, b16),
            pltpu.VMEM(w_up.shape, b16),
            pltpu.VMEM(w_down.shape, b16),
            pltpu.VMEM((batch * heads, lanes), f32),
            pltpu.VMEM((batch * heads, ctx), f32),
            pltpu.VMEM((batch * heads, lanes), f32),
            pltpu.VMEM((batch * heads, lanes), f32),
            pltpu.VMEM((shards, batch, width), b16),
            pltpu.VMEM((shards, batch, lanes), f32),
            pltpu.VMEM((shards, 8, cols), f32),
            pltpu.VMEM((tps, batch, cols), f32),
            pltpu.VMEM((shards, batch, cols), b16),
            pltpu.VMEM((shards, batch, cols), b16),
            pltpu.VMEM((shards, batch, cols), b16),
            pltpu.VMEM((tps, batch, cols), f32),
            sems(7), sems(k), sems(k), sems(k), sems(k), sems(k), sems(k),
            sems(t), sems(t), sems(k), sems(k), sems(k), sems(k), sems(t), sems(t),
        ],
        compiler_params=pltpu.CompilerParams(
            collective_id=0, has_side_effects=True, vmem_limit_bytes=60 * 1024 * 1024
        ),
    )(
        queries, keys, values, lengths, out_weight, residual, norm_gain,
        expert_ids.T, gate_probs.T, w_gate, w_up, w_down,
    ))


def body(queries, keys, values, lengths, out_weight, residual, norm_gain, expert_ids, gate_probs, w_gate, w_up, w_down):
    args = (queries, keys, values, lengths, out_weight, residual, norm_gain, expert_ids, gate_probs, w_gate, w_up, w_down)
    fits = (
        keys.shape[1] == 128
        and keys.shape[2] == 2 * HEAD
        and w_gate.shape[0] == 1
        and residual.shape[1] % 128 == 0
        and queries.shape[0] % 16 == 0
        and (queries.shape[1] // HEAD) % 16 == 0
    )
    return on_device_fused(*args) if fits else on_device(*args)


def solution(mesh):
    return jax.shard_map(
        body,
        mesh=mesh,
        in_specs=(
            P("grp", "tp"),
            P("grp", "kvp", "tp"),
            P("grp", "kvp", "tp"),
            P("grp"),
            P("tp", "kvp"),
            P("grp", "kvp"),
            P("kvp"),
            P("grp", None),
            P("grp", None),
            P("kvp", None, "tp"),
            P("kvp", None, "tp"),
            P("kvp", "tp", None),
        ),
        out_specs=(P("grp", "tp"), P("grp", "kvp")),
        check_vma=False,
    )
```

```python
import jax
import jax.numpy as jnp
from jax import lax
from jax.experimental import pallas as pl
from jax.experimental.pallas import tpu as pltpu
from jax.sharding import PartitionSpec as P

MESH = pl.DeviceIdType.MESH

D = 1536
HEAD = 64


EPSILON = 1e-05
NEGATIVE = -1e30


def merged(part, axis, combine):
    gathered = jax.tree.map(lambda a: lax.all_gather(a, axis), part)

    def take(source):
        return jax.tree.map(lambda a: lax.dynamic_index_in_dim(a, source, 0, False), gathered)

    return lax.fori_loop(
        1, lax.axis_size(axis), lambda source, state: combine(state, take(source)), take(0)
    )


def slot_tables(expert_ids, gate_probs, experts, capacity):
    batch_size, top_count = expert_ids.shape
    flat_ids = expert_ids.reshape(-1)
    pair_count = flat_ids.shape[0]
    pair_order = jnp.arange(pair_count, dtype=jnp.int32)
    earlier_same = (flat_ids[:, None] == flat_ids[None, :]) & (
        pair_order[None, :] < pair_order[:, None]
    )
    slot_index = jnp.sum(earlier_same.astype(jnp.int32), axis=1)
    target_col = flat_ids * capacity + slot_index
    columns = jnp.arange(experts * capacity, dtype=jnp.int32)
    hit_table = (target_col[:, None] == columns[None, :]).astype(jnp.float32)
    hit_table = hit_table.reshape(batch_size, top_count, experts * capacity)
    dispatch = jnp.sum(hit_table, axis=1)
    combine = jnp.sum(hit_table * gate_probs[:, :, None], axis=1)
    return (dispatch, combine)


def merge_partial(earlier, latest):
    global_max = jnp.maximum(earlier[0], latest[0])
    lead_scale = jnp.exp(earlier[0] - global_max)
    trail_scale = jnp.exp(latest[0] - global_max)
    return (
        global_max,
        lead_scale * earlier[1] + trail_scale * latest[1],
        lead_scale[..., None] * earlier[2] + trail_scale[..., None] * latest[2],
    )


def on_device(
    queries,
    keys,
    values,
    lengths,
    out_weight,
    residual,
    norm_gain,
    expert_ids,
    gate_probs,
    w_gate,
    w_up,
    w_down,
):
    batch_size = queries.shape[0]
    local_kv = keys.shape[2] // HEAD
    local_heads = queries.shape[1] // HEAD
    group_size = local_heads // local_kv
    ctx_dev = keys.shape[1]
    shards = lax.axis_size("kvp")
    query_heads = queries.reshape(batch_size, local_kv, group_size, HEAD)
    key_rows = keys.reshape(batch_size, ctx_dev, local_kv, HEAD)
    value_rows = values.reshape(batch_size, ctx_dev, local_kv, HEAD)
    scores = jnp.einsum(
        "bgrd,bcgd->bgrc", query_heads, key_rows, preferred_element_type=jnp.float32
    ) * HEAD ** (-0.5)
    position = lax.axis_index("kvp") * ctx_dev + jnp.arange(ctx_dev, dtype=jnp.int32)
    valid_key = (position[None, :] < lengths[:, None])[:, None, None, :]
    masked = jnp.where(valid_key, scores, NEGATIVE)
    block_max = jnp.max(masked, axis=3)
    weights = jnp.where(valid_key, jnp.exp(masked - block_max[..., None]), 0.0)
    rounded = weights.astype(jnp.bfloat16)
    block_sum = jnp.sum(rounded.astype(jnp.float32), axis=3)
    block_out = jnp.einsum(
        "bgrc,bcgd->bgrd", rounded, value_rows, preferred_element_type=jnp.float32
    )
    global_max, denominator, summed = merged(
        (block_max, block_sum, block_out), "kvp", merge_partial
    )
    attended = (summed / denominator[..., None]).reshape(batch_size, local_heads * HEAD)
    projected = lax.psum(
        jnp.dot(attended.astype(jnp.bfloat16), out_weight, preferred_element_type=jnp.float32), "tp"
    )
    hidden_state = lax.optimization_barrier(
        (projected + residual.astype(jnp.float32)).astype(jnp.bfloat16)
    )
    state_wide = hidden_state.astype(jnp.float32)
    col_count = hidden_state.shape[1]
    exp_dev = w_gate.shape[0]
    experts = exp_dev * shards
    capacity = min(batch_size, max(2, 2 * batch_size * expert_ids.shape[1] // experts))
    dispatch, combine = slot_tables(expert_ids, gate_probs, experts, capacity)
    total_sq = lax.psum(jnp.sum(state_wide * state_wide, axis=1), "kvp")
    inverse = lax.rsqrt(total_sq / D + EPSILON)
    normed = (state_wide * inverse[:, None] * norm_gain.astype(jnp.float32)[None, :]).astype(
        jnp.bfloat16
    )
    outgoing = jnp.dot(
        dispatch.T.astype(jnp.bfloat16), normed, preferred_element_type=jnp.float32
    ).astype(jnp.bfloat16)
    outgoing = outgoing.reshape(experts, capacity, col_count)
    expert_rows = lax.all_to_all(outgoing, "kvp", split_axis=0, concat_axis=2, tiled=True)
    gate_proj = jnp.einsum("ecd,edf->ecf", expert_rows, w_gate, preferred_element_type=jnp.float32)
    up_proj = jnp.einsum("ecd,edf->ecf", expert_rows, w_up, preferred_element_type=jnp.float32)
    activation = (jax.nn.silu(gate_proj) * up_proj).astype(jnp.bfloat16)
    partial_value = jnp.einsum(
        "ecf,efd->ecd", activation, w_down, preferred_element_type=jnp.float32
    )
    returned = lax.all_to_all(partial_value, "kvp", split_axis=2, concat_axis=0, tiled=True)
    moe_local = jnp.dot(
        combine, returned.reshape(experts * capacity, col_count), precision=lax.Precision.HIGHEST
    )
    moe_term = lax.psum(moe_local, "tp")
    mixed = (state_wide + moe_term).astype(jnp.bfloat16)
    return (attended, mixed)


NORM_WIDTH = D


def peers(axis):
    count = lax.axis_size(axis)
    me = lax.axis_index(axis)
    return [(step - 1, lax.rem(me + step, count)) for step in range(1, count)]


def fused(
    q_hbm, k_hbm, v_hbm, len_hbm, wo_hbm, res_hbm, gain_hbm, ids_hbm, gp_hbm, wg_hbm, wu_hbm, wd_hbm,
    att_ref, mix_ref,
    q_vm, k_vm, v_vm, len_ref, wo_vm, res_ref, gain_ref, ids_ref, gp_ref, wg_vm, wu_vm, wd_vm,
    q_rows, s_rows, o_rows, t_rows,
    o_all, stat_all, gain_all, p_all, h_all, y_send, y_recv, z_all,
    load_sem, o_send, o_recv, st_send, st_recv, g_send, g_recv,
    p_send, p_recv, h_send, h_recv, ys_send, ys_recv, z_send, z_recv,
):
    shards = o_all.shape[0]
    tps = p_all.shape[0]
    batch, width = q_vm.shape
    heads = width // HEAD
    ctx = k_vm.shape[1]
    lanes = k_vm.shape[2]
    cols = wo_vm.shape[1]
    group = heads * HEAD // lanes
    mine = lax.axis_index("kvp")
    my_tp = lax.axis_index("tp")
    kvp_peers = peers("kvp")
    tp_peers = peers("tp")

    barrier = pltpu.get_barrier_semaphore()
    for _, peer in kvp_peers:
        pl.semaphore_signal(barrier, inc=1, device_id={"kvp": peer}, device_id_type=MESH)
    for _, peer in tp_peers:
        pl.semaphore_signal(barrier, inc=1, device_id={"tp": peer}, device_id_type=MESH)

    def load(index, source, target):
        return pltpu.make_async_copy(source, target, load_sem.at[index])

    len_load = load(0, len_hbm, len_ref)
    q_load = load(1, q_hbm, q_vm)
    k_load = load(2, k_hbm, k_vm)
    v_load = load(3, v_hbm, v_vm)
    res_load = load(4, res_hbm, res_ref)
    gain_load = load(5, gain_hbm, gain_ref)
    ids_load = load(6, ids_hbm, ids_ref)
    gp_load = load(7, gp_hbm, gp_ref)
    wo_load = load(8, wo_hbm, wo_vm)
    wg_load = load(9, wg_hbm, wg_vm)
    wu_load = load(10, wu_hbm, wu_vm)
    wd_load = load(11, wd_hbm, wd_vm)
    for copy in (q_load, len_load, k_load, v_load, gain_load, res_load, ids_load, gp_load):
        copy.start()

    sent = []

    def push(source, target, send, recv, place):
        copy = pltpu.make_async_remote_copy(
            src_ref=source, dst_ref=target, send_sem=send, recv_sem=recv,
            device_id=place, device_id_type=MESH,
        )
        copy.start()
        sent.append(copy)
        return copy

    lane = lax.broadcasted_iota(jnp.int32, (batch, lanes), 1)
    low = lane < HEAD

    q_load.wait()
    for head in range(heads):
        pair = head // 2
        wide = q_vm[:, pair * lanes : (pair + 1) * lanes].astype(jnp.float32)
        kept = jnp.where(low if head % 2 == 0 else ~low, wide, 0.0)
        if head % 2 != head // group:
            kept = pltpu.roll(kept, HEAD, 1)
        q_rows[pl.ds(head, batch, stride=heads), :] = kept

    len_load.wait()
    k_load.wait()
    wo_load.start()
    position = mine * ctx + lax.broadcasted_iota(jnp.int32, (heads, ctx), 1)
    for b in range(batch):
        rows = pl.ds(b * heads, heads)
        scores = lax.dot_general(
            q_rows[rows, :].astype(jnp.bfloat16), k_vm[b],
            (((1,), (1,)), ((), ())), preferred_element_type=jnp.float32,
        ) * HEAD ** (-0.5)
        s_rows[rows, :] = jnp.where(position < len_ref[b], scores, NEGATIVE)
    v_load.wait()
    wg_load.start()
    wu_load.start()
    wd_load.start()
    stat_low = lax.broadcasted_iota(jnp.int32, (heads, lanes), 1) < HEAD
    for b in range(batch):
        rows = pl.ds(b * heads, heads)
        masked = s_rows[rows, :]
        block_max = jnp.max(masked, axis=1, keepdims=True)
        weights = jnp.where(position < len_ref[b], jnp.exp(masked - block_max), 0.0)
        rounded = weights.astype(jnp.bfloat16)
        block_sum = jnp.sum(rounded.astype(jnp.float32), axis=1, keepdims=True)
        out = jnp.dot(rounded, v_vm[b], preferred_element_type=jnp.float32)
        o_rows[pl.ds(b, heads, stride=batch), :] = out
        t_rows[pl.ds(b, heads, stride=batch), :] = jnp.where(stat_low, block_max, block_sum)
    stat = jnp.ones((batch, lanes), jnp.float32)
    for pair in range(heads // 2):
        first = o_rows[2 * pair * batch : (2 * pair + 1) * batch, :]
        second = o_rows[(2 * pair + 1) * batch : (2 * pair + 2) * batch, :]
        if 2 * pair // group == 0:
            second = pltpu.roll(second, HEAD, 1)
        else:
            first = pltpu.roll(first, HEAD, 1)
        o_all[mine, :, pair * lanes : (pair + 1) * lanes] = jnp.where(low, first, second).astype(jnp.bfloat16)
    for head in range(heads):
        stat = jnp.where((lane == head) | (lane == HEAD + head), t_rows[head * batch : (head + 1) * batch, :], stat)
    stat_all[mine] = stat

    gain_load.wait()
    gain_all[mine] = jnp.broadcast_to(gain_ref[...].astype(jnp.float32).reshape(1, cols), (8, cols))
    pl.semaphore_wait(barrier, len(kvp_peers) + len(tp_peers))
    o_copies = []
    for slot, peer in kvp_peers:
        o_copies.append(push(stat_all.at[mine], stat_all.at[mine], st_send.at[slot], st_recv.at[slot], {"kvp": peer}))
        o_copies.append(push(o_all.at[mine], o_all.at[mine], o_send.at[slot], o_recv.at[slot], {"kvp": peer}))
    g_copies = [
        push(gain_all.at[mine], gain_all.at[mine], g_send.at[slot], g_recv.at[slot], {"kvp": peer})
        for slot, peer in kvp_peers
    ]
    for copy in (wo_load, res_load, ids_load, gp_load):
        copy.wait()
    for copy in o_copies:
        copy.wait_recv()

    global_max = stat_all[0]
    for s in range(1, shards):
        global_max = jnp.maximum(global_max, stat_all[s])
    scales = []
    denominator = None
    for s in range(shards):
        stat = stat_all[s]
        scale = jnp.exp(stat - global_max)
        scales.append(scale)
        term = scale * pltpu.roll(stat, HEAD, 1)
        denominator = term if denominator is None else denominator + term
    inverse = 1.0 / denominator
    factors = [scale * inverse for scale in scales]
    parts = []
    for pair in range(heads // 2):
        block = slice(pair * lanes, (pair + 1) * lanes)
        total = None
        for s in range(shards):
            spread = jnp.where(
                low,
                jnp.broadcast_to(factors[s][:, 2 * pair : 2 * pair + 1], (batch, lanes)),
                jnp.broadcast_to(factors[s][:, 2 * pair + 1 : 2 * pair + 2], (batch, lanes)),
            )
            term = spread * o_all[s, :, block].astype(jnp.float32)
            total = term if total is None else total + term
        att_ref[:, block] = total
        parts.append(total.astype(jnp.bfloat16))
    attended = jnp.concatenate(parts, axis=1)

    p_all[my_tp] = jnp.dot(attended, wo_vm[...], preferred_element_type=jnp.float32)
    p_copies = [
        push(p_all.at[my_tp], p_all.at[my_tp], p_send.at[slot], p_recv.at[slot], {"tp": peer})
        for slot, peer in tp_peers
    ]
    gate_row = jnp.sum(jnp.where(ids_ref[...] == mine, gp_ref[...], 0.0), axis=0, keepdims=True)
    square = (batch, batch)
    diagonal = lax.broadcasted_iota(jnp.int32, square, 0) == lax.broadcasted_iota(jnp.int32, square, 1)
    expert_gate = jnp.sum(jnp.where(diagonal, jnp.broadcast_to(gate_row, square), 0.0), axis=1, keepdims=True)
    for copy in p_copies:
        copy.wait_recv()
    projected = p_all[0]
    for s in range(1, tps):
        projected = projected + p_all[s]
    hidden = (projected + res_ref[...].astype(jnp.float32)).astype(jnp.bfloat16)
    h_all[mine] = hidden
    h_copies = [
        push(h_all.at[mine], h_all.at[mine], h_send.at[slot], h_recv.at[slot], {"kvp": peer})
        for slot, peer in kvp_peers
    ]
    wg_load.wait()
    wu_load.wait()
    wd_load.wait()
    for copy in g_copies:
        copy.wait_recv()
    for copy in h_copies:
        copy.wait_recv()

    states = [h_all[s].astype(jnp.float32) for s in range(shards)]
    squares = None
    for state in states:
        term = state * state
        squares = term if squares is None else squares + term
    root = lax.rsqrt(jnp.sum(squares, axis=1, keepdims=True) / NORM_WIDTH + EPSILON)
    normed = jnp.concatenate(
        [(states[s] * root * gain_all[s, 0:1, :]).astype(jnp.bfloat16) for s in range(shards)], axis=1
    )
    gate_proj = jnp.dot(normed, wg_vm[0], preferred_element_type=jnp.float32)
    up_proj = jnp.dot(normed, wu_vm[0], preferred_element_type=jnp.float32)
    activation = (gate_proj / (1.0 + jnp.exp(-gate_proj)) * up_proj).astype(jnp.bfloat16)
    expert_out = jnp.dot(activation, wd_vm[0], preferred_element_type=jnp.float32) * expert_gate
    for s in range(shards):
        y_send[s] = expert_out[:, s * cols : (s + 1) * cols].astype(y_send.dtype)
    y_copies = [
        push(y_send.at[peer], y_recv.at[mine], ys_send.at[slot], ys_recv.at[slot], {"kvp": peer})
        for slot, peer in kvp_peers
    ]
    y_recv[mine] = y_send[mine]
    for copy in y_copies:
        copy.wait_recv()
    term = y_recv[0].astype(jnp.float32)
    for s in range(1, shards):
        term = term + y_recv[s].astype(jnp.float32)
    z_all[my_tp] = term.astype(z_all.dtype)
    z_copies = [
        push(z_all.at[my_tp], z_all.at[my_tp], z_send.at[slot], z_recv.at[slot], {"tp": peer})
        for slot, peer in tp_peers
    ]
    for copy in z_copies:
        copy.wait_recv()
    moe = z_all[0].astype(jnp.float32)
    for s in range(1, tps):
        moe = moe + z_all[s].astype(jnp.float32)
    mix_ref[...] = (hidden.astype(jnp.float32) + moe).astype(jnp.bfloat16)
    for copy in sent:
        copy.wait_send()


def on_device_fused(
    queries, keys, values, lengths, out_weight, residual, norm_gain, expert_ids, gate_probs, w_gate, w_up, w_down
):
    shards = lax.axis_size("kvp")
    tps = lax.axis_size("tp")
    batch, width = queries.shape
    heads = width // HEAD
    ctx, lanes = keys.shape[1:]
    cols = residual.shape[1]
    vmem = pl.BlockSpec(memory_space=pltpu.VMEM)
    anywhere = pl.BlockSpec(memory_space=pl.ANY)
    f32, b16 = jnp.float32, jnp.bfloat16

    def sems(count):
        return pltpu.SemaphoreType.DMA((max(count, 1),))

    k, t = shards - 1, tps - 1
    return tuple(pl.pallas_call(
        fused,
        out_shape=(
            pltpu.VMEM((batch, width), f32),
            pltpu.VMEM((batch, cols), b16),
        ),
        in_specs=[anywhere] * 12,
        out_specs=(vmem, vmem),
        scratch_shapes=[
            pltpu.VMEM(queries.shape, b16),
            pltpu.VMEM(keys.shape, b16),
            pltpu.VMEM(values.shape, b16),
            pltpu.SMEM(lengths.shape, jnp.int32),
            pltpu.VMEM(out_weight.shape, b16),
            pltpu.VMEM(residual.shape, b16),
            pltpu.VMEM(norm_gain.shape, b16),
            pltpu.VMEM(expert_ids.shape[::-1], jnp.int32),
            pltpu.VMEM(gate_probs.shape[::-1], f32),
            pltpu.VMEM(w_gate.shape, b16),
            pltpu.VMEM(w_up.shape, b16),
            pltpu.VMEM(w_down.shape, b16),
            pltpu.VMEM((batch * heads, lanes), f32),
            pltpu.VMEM((batch * heads, ctx), f32),
            pltpu.VMEM((batch * heads, lanes), f32),
            pltpu.VMEM((batch * heads, lanes), f32),
            pltpu.VMEM((shards, batch, width), b16),
            pltpu.VMEM((shards, batch, lanes), f32),
            pltpu.VMEM((shards, 8, cols), f32),
            pltpu.VMEM((tps, batch, cols), f32),
            pltpu.VMEM((shards, batch, cols), b16),
            pltpu.VMEM((shards, batch, cols), b16),
            pltpu.VMEM((shards, batch, cols), b16),
            pltpu.VMEM((tps, batch, cols), f32),
            sems(12), sems(k), sems(k), sems(k), sems(k), sems(k), sems(k),
            sems(t), sems(t), sems(k), sems(k), sems(k), sems(k), sems(t), sems(t),
        ],
        compiler_params=pltpu.CompilerParams(
            collective_id=0, has_side_effects=True, vmem_limit_bytes=60 * 1024 * 1024
        ),
    )(
        queries, keys, values, lengths, out_weight, residual, norm_gain,
        expert_ids.T, gate_probs.T, w_gate, w_up, w_down,
    ))


def body(queries, keys, values, lengths, out_weight, residual, norm_gain, expert_ids, gate_probs, w_gate, w_up, w_down):
    args = (queries, keys, values, lengths, out_weight, residual, norm_gain, expert_ids, gate_probs, w_gate, w_up, w_down)
    fits = (
        keys.shape[1] == 128
        and keys.shape[2] == 2 * HEAD
        and w_gate.shape[0] == 1
        and residual.shape[1] % 128 == 0
        and queries.shape[0] % 16 == 0
        and (queries.shape[1] // HEAD) % 16 == 0
    )
    return on_device_fused(*args) if fits else on_device(*args)


def solution(mesh):
    return jax.shard_map(
        body,
        mesh=mesh,
        in_specs=(
            P("grp", "tp"),
            P("grp", "kvp", "tp"),
            P("grp", "kvp", "tp"),
            P("grp"),
            P("tp", "kvp"),
            P("grp", "kvp"),
            P("kvp"),
            P("grp", None),
            P("grp", None),
            P("kvp", None, "tp"),
            P("kvp", None, "tp"),
            P("kvp", "tp", None),
        ),
        out_specs=(P("grp", "tp"), P("grp", "kvp")),
        check_vma=False,
    )
```

```python
import functools

import jax
import jax.numpy as jnp
from jax import lax
from jax.experimental import pallas as pl
from jax.experimental.pallas import tpu as pltpu
from jax.sharding import PartitionSpec as P

MESH = pl.DeviceIdType.MESH

D = 1536
HEAD = 64


EPSILON = 1e-05
NEGATIVE = -1e30


def merged(part, axis, combine):
    gathered = jax.tree.map(lambda a: lax.all_gather(a, axis), part)

    def take(source):
        return jax.tree.map(lambda a: lax.dynamic_index_in_dim(a, source, 0, False), gathered)

    return lax.fori_loop(
        1, lax.axis_size(axis), lambda source, state: combine(state, take(source)), take(0)
    )


def slot_tables(expert_ids, gate_probs, experts, capacity):
    batch_size, top_count = expert_ids.shape
    flat_ids = expert_ids.reshape(-1)
    pair_count = flat_ids.shape[0]
    pair_order = jnp.arange(pair_count, dtype=jnp.int32)
    earlier_same = (flat_ids[:, None] == flat_ids[None, :]) & (
        pair_order[None, :] < pair_order[:, None]
    )
    slot_index = jnp.sum(earlier_same.astype(jnp.int32), axis=1)
    target_col = flat_ids * capacity + slot_index
    columns = jnp.arange(experts * capacity, dtype=jnp.int32)
    hit_table = (target_col[:, None] == columns[None, :]).astype(jnp.float32)
    hit_table = hit_table.reshape(batch_size, top_count, experts * capacity)
    dispatch = jnp.sum(hit_table, axis=1)
    combine = jnp.sum(hit_table * gate_probs[:, :, None], axis=1)
    return (dispatch, combine)


def merge_partial(earlier, latest):
    global_max = jnp.maximum(earlier[0], latest[0])
    lead_scale = jnp.exp(earlier[0] - global_max)
    trail_scale = jnp.exp(latest[0] - global_max)
    return (
        global_max,
        lead_scale * earlier[1] + trail_scale * latest[1],
        lead_scale[..., None] * earlier[2] + trail_scale[..., None] * latest[2],
    )


def on_device(
    queries,
    keys,
    values,
    lengths,
    out_weight,
    residual,
    norm_gain,
    expert_ids,
    gate_probs,
    w_gate,
    w_up,
    w_down,
):
    batch_size = queries.shape[0]
    local_kv = keys.shape[2] // HEAD
    local_heads = queries.shape[1] // HEAD
    group_size = local_heads // local_kv
    ctx_dev = keys.shape[1]
    shards = lax.axis_size("kvp")
    query_heads = queries.reshape(batch_size, local_kv, group_size, HEAD)
    key_rows = keys.reshape(batch_size, ctx_dev, local_kv, HEAD)
    value_rows = values.reshape(batch_size, ctx_dev, local_kv, HEAD)
    scores = jnp.einsum(
        "bgrd,bcgd->bgrc", query_heads, key_rows, preferred_element_type=jnp.float32
    ) * HEAD ** (-0.5)
    position = lax.axis_index("kvp") * ctx_dev + jnp.arange(ctx_dev, dtype=jnp.int32)
    valid_key = (position[None, :] < lengths[:, None])[:, None, None, :]
    masked = jnp.where(valid_key, scores, NEGATIVE)
    block_max = jnp.max(masked, axis=3)
    weights = jnp.where(valid_key, jnp.exp(masked - block_max[..., None]), 0.0)
    rounded = weights.astype(jnp.bfloat16)
    block_sum = jnp.sum(rounded.astype(jnp.float32), axis=3)
    block_out = jnp.einsum(
        "bgrc,bcgd->bgrd", rounded, value_rows, preferred_element_type=jnp.float32
    )
    global_max, denominator, summed = merged(
        (block_max, block_sum, block_out), "kvp", merge_partial
    )
    attended = (summed / denominator[..., None]).reshape(batch_size, local_heads * HEAD)
    projected = lax.psum(
        jnp.dot(attended.astype(jnp.bfloat16), out_weight, preferred_element_type=jnp.float32), "tp"
    )
    hidden_state = lax.optimization_barrier(
        (projected + residual.astype(jnp.float32)).astype(jnp.bfloat16)
    )
    state_wide = hidden_state.astype(jnp.float32)
    col_count = hidden_state.shape[1]
    exp_dev = w_gate.shape[0]
    experts = exp_dev * shards
    capacity = min(batch_size, max(2, 2 * batch_size * expert_ids.shape[1] // experts))
    dispatch, combine = slot_tables(expert_ids, gate_probs, experts, capacity)
    total_sq = lax.psum(jnp.sum(state_wide * state_wide, axis=1), "kvp")
    inverse = lax.rsqrt(total_sq / D + EPSILON)
    normed = (state_wide * inverse[:, None] * norm_gain.astype(jnp.float32)[None, :]).astype(
        jnp.bfloat16
    )
    outgoing = jnp.dot(
        dispatch.T.astype(jnp.bfloat16), normed, preferred_element_type=jnp.float32
    ).astype(jnp.bfloat16)
    outgoing = outgoing.reshape(experts, capacity, col_count)
    expert_rows = lax.all_to_all(outgoing, "kvp", split_axis=0, concat_axis=2, tiled=True)
    gate_proj = jnp.einsum("ecd,edf->ecf", expert_rows, w_gate, preferred_element_type=jnp.float32)
    up_proj = jnp.einsum("ecd,edf->ecf", expert_rows, w_up, preferred_element_type=jnp.float32)
    activation = (jax.nn.silu(gate_proj) * up_proj).astype(jnp.bfloat16)
    partial_value = jnp.einsum(
        "ecf,efd->ecd", activation, w_down, preferred_element_type=jnp.float32
    )
    returned = lax.all_to_all(partial_value, "kvp", split_axis=2, concat_axis=0, tiled=True)
    moe_local = jnp.dot(
        combine, returned.reshape(experts * capacity, col_count), precision=lax.Precision.HIGHEST
    )
    moe_term = lax.psum(moe_local, "tp")
    mixed = (state_wide + moe_term).astype(jnp.bfloat16)
    return (attended, mixed)


NORM_WIDTH = D


def peers(axis):
    count = lax.axis_size(axis)
    me = lax.axis_index(axis)
    return [(step - 1, lax.rem(me + step, count)) for step in range(1, count)]


def fused(
    q_hbm, k_hbm, v_hbm, len_hbm, wo_hbm, res_hbm, gain_hbm, ids_hbm, gp_hbm, wg_hbm, wu_hbm, wd_hbm,
    att_ref, mix_ref,
    q_vm, k_vm, v_vm, len_ref, wo_vm, res_ref, gain_ref, ids_ref, gp_ref, wg_vm, wu_vm, wd_vm,
    q_rows, s_rows, o_rows, t_rows,
    o_all, stat_all, gain_all, p_all, h_all, y_send, y_recv, z_all,
    load_sem, o_send, o_recv, st_send, st_recv, g_send, g_recv,
    p_send, p_recv, h_send, h_recv, ys_send, ys_recv, z_send, z_recv,
):
    shards = o_all.shape[0]
    tps = p_all.shape[0]
    batch, width = q_vm.shape
    heads = width // HEAD
    ctx = k_vm.shape[1]
    lanes = k_vm.shape[2]
    cols = wo_vm.shape[1]
    group = heads * HEAD // lanes
    mine = lax.axis_index("kvp")
    my_tp = lax.axis_index("tp")
    kvp_peers = peers("kvp")
    tp_peers = peers("tp")

    barrier = pltpu.get_barrier_semaphore()
    for _, peer in kvp_peers:
        pl.semaphore_signal(barrier, inc=1, device_id={"kvp": peer}, device_id_type=MESH)
    for _, peer in tp_peers:
        pl.semaphore_signal(barrier, inc=1, device_id={"tp": peer}, device_id_type=MESH)

    def load(index, source, target):
        return pltpu.make_async_copy(source, target, load_sem.at[index])

    len_load = load(0, len_hbm, len_ref)
    q_load = load(1, q_hbm, q_vm)
    k_load = load(2, k_hbm, k_vm)
    v_load = load(3, v_hbm, v_vm)
    res_load = load(4, res_hbm, res_ref)
    gain_load = load(5, gain_hbm, gain_ref)
    ids_load = load(6, ids_hbm, ids_ref)
    gp_load = load(7, gp_hbm, gp_ref)
    wo_load = load(8, wo_hbm, wo_vm)
    wg_load = load(9, wg_hbm, wg_vm)
    wu_load = load(10, wu_hbm, wu_vm)
    wd_load = load(11, wd_hbm, wd_vm)
    for copy in (q_load, len_load, k_load, v_load, gain_load, res_load, ids_load, gp_load):
        copy.start()

    sent = []

    def push(source, target, send, recv, place):
        copy = pltpu.make_async_remote_copy(
            src_ref=source, dst_ref=target, send_sem=send, recv_sem=recv,
            device_id=place, device_id_type=MESH,
        )
        copy.start()
        sent.append(copy)
        return copy

    lane = lax.broadcasted_iota(jnp.int32, (batch, lanes), 1)
    low = lane < HEAD

    q_load.wait()
    for head in range(heads):
        pair = head // 2
        wide = q_vm[:, pair * lanes : (pair + 1) * lanes].astype(jnp.float32)
        kept = jnp.where(low if head % 2 == 0 else ~low, wide, 0.0)
        if head % 2 != head // group:
            kept = pltpu.roll(kept, HEAD, 1)
        q_rows[pl.ds(head, batch, stride=heads), :] = kept

    len_load.wait()
    k_load.wait()
    wo_load.start()
    position = mine * ctx + lax.broadcasted_iota(jnp.int32, (heads, ctx), 1)
    for b in range(batch):
        rows = pl.ds(b * heads, heads)
        scores = lax.dot_general(
            q_rows[rows, :].astype(jnp.bfloat16), k_vm[b],
            (((1,), (1,)), ((), ())), preferred_element_type=jnp.float32,
        ) * HEAD ** (-0.5)
        s_rows[rows, :] = jnp.where(position < len_ref[b], scores, NEGATIVE)
    v_load.wait()
    wg_load.start()
    wu_load.start()
    wd_load.start()
    stat_low = lax.broadcasted_iota(jnp.int32, (heads, lanes), 1) < HEAD
    for b in range(batch):
        rows = pl.ds(b * heads, heads)
        masked = s_rows[rows, :]
        block_max = jnp.max(masked, axis=1, keepdims=True)
        weights = jnp.where(position < len_ref[b], jnp.exp(masked - block_max), 0.0)
        rounded = weights.astype(jnp.bfloat16)
        block_sum = jnp.sum(rounded.astype(jnp.float32), axis=1, keepdims=True)
        out = jnp.dot(rounded, v_vm[b], preferred_element_type=jnp.float32)
        o_rows[pl.ds(b, heads, stride=batch), :] = out
        t_rows[pl.ds(b, heads, stride=batch), :] = jnp.where(stat_low, block_max, block_sum)
    stat = jnp.ones((batch, lanes), jnp.float32)
    for pair in range(heads // 2):
        first = o_rows[2 * pair * batch : (2 * pair + 1) * batch, :]
        second = o_rows[(2 * pair + 1) * batch : (2 * pair + 2) * batch, :]
        if 2 * pair // group == 0:
            second = pltpu.roll(second, HEAD, 1)
        else:
            first = pltpu.roll(first, HEAD, 1)
        o_all[mine, :, pair * lanes : (pair + 1) * lanes] = jnp.where(low, first, second).astype(jnp.bfloat16)
    for head in range(heads):
        stat = jnp.where((lane == head) | (lane == HEAD + head), t_rows[head * batch : (head + 1) * batch, :], stat)
    half = batch // 2
    fold = lax.rem(lane[:half], HEAD) < heads
    stat_all[mine] = jnp.where(fold, stat[:half], pltpu.roll(stat[half:], heads, 1))

    gain_load.wait()
    gain_all[mine] = jnp.broadcast_to(gain_ref[...].astype(jnp.float32).reshape(1, cols), (1, cols))
    pl.semaphore_wait(barrier, len(kvp_peers) + len(tp_peers))
    o_copies = []
    for slot, peer in kvp_peers:
        o_copies.append(push(stat_all.at[mine], stat_all.at[mine], st_send.at[slot], st_recv.at[slot], {"kvp": peer}))
        o_copies.append(push(o_all.at[mine], o_all.at[mine], o_send.at[slot], o_recv.at[slot], {"kvp": peer}))
    for copy in (wo_load, res_load, ids_load, gp_load):
        copy.wait()
    for copy in o_copies:
        copy.wait_recv()

    stats = [
        jnp.concatenate([stat_all[s], pltpu.roll(stat_all[s], lanes - heads, 1)], axis=0) for s in range(shards)
    ]
    global_max = functools.reduce(jnp.maximum, stats)
    scales = []
    denominator = None
    for s in range(shards):
        stat = stats[s]
        scale = jnp.exp(stat - global_max)
        scales.append(scale)
        term = scale * pltpu.roll(stat, HEAD, 1)
        denominator = term if denominator is None else denominator + term
    inverse = 1.0 / denominator
    factors = [scale * inverse for scale in scales]
    parts = []
    for pair in range(heads // 2):
        block = slice(pair * lanes, (pair + 1) * lanes)
        total = None
        for s in range(shards):
            spread = jnp.where(
                low,
                jnp.broadcast_to(factors[s][:, 2 * pair : 2 * pair + 1], (batch, lanes)),
                jnp.broadcast_to(factors[s][:, 2 * pair + 1 : 2 * pair + 2], (batch, lanes)),
            )
            term = spread * o_all[s, :, block].astype(jnp.float32)
            total = term if total is None else total + term
        att_ref[:, block] = total
        parts.append(total.astype(jnp.bfloat16))
    attended = jnp.concatenate(parts, axis=1)

    p_all[my_tp] = jnp.dot(attended, wo_vm[...], preferred_element_type=jnp.float32)
    p_copies = [
        push(p_all.at[my_tp], p_all.at[my_tp], p_send.at[slot], p_recv.at[slot], {"tp": peer})
        for slot, peer in tp_peers
    ]
    g_copies = [
        push(gain_all.at[mine], gain_all.at[mine], g_send.at[slot], g_recv.at[slot], {"kvp": peer})
        for slot, peer in kvp_peers
    ]
    gate_row = jnp.sum(jnp.where(ids_ref[...] == mine, gp_ref[...], 0.0), axis=0, keepdims=True)
    square = (batch, batch)
    diagonal = lax.broadcasted_iota(jnp.int32, square, 0) == lax.broadcasted_iota(jnp.int32, square, 1)
    expert_gate = jnp.sum(jnp.where(diagonal, jnp.broadcast_to(gate_row, square), 0.0), axis=1, keepdims=True)
    for copy in p_copies:
        copy.wait_recv()
    projected = p_all[0]
    for s in range(1, tps):
        projected = projected + p_all[s]
    hidden = (projected + res_ref[...].astype(jnp.float32)).astype(jnp.bfloat16)
    h_all[mine] = hidden
    h_copies = [
        push(h_all.at[mine], h_all.at[mine], h_send.at[slot], h_recv.at[slot], {"kvp": peer})
        for slot, peer in kvp_peers
    ]
    wg_load.wait()
    wu_load.wait()
    wd_load.wait()
    for copy in g_copies:
        copy.wait_recv()
    for copy in h_copies:
        copy.wait_recv()

    states = [h_all[s].astype(jnp.float32) for s in range(shards)]
    squares = None
    for state in states:
        term = state * state
        squares = term if squares is None else squares + term
    root = lax.rsqrt(jnp.sum(squares, axis=1, keepdims=True) / NORM_WIDTH + EPSILON)
    normed = jnp.concatenate(
        [(states[s] * root * gain_all[s, 0:1, :]).astype(jnp.bfloat16) for s in range(shards)], axis=1
    )
    gate_proj = jnp.dot(normed, wg_vm[0], preferred_element_type=jnp.float32)
    up_proj = jnp.dot(normed, wu_vm[0], preferred_element_type=jnp.float32)
    activation = (gate_proj / (1.0 + jnp.exp(-gate_proj)) * up_proj).astype(jnp.bfloat16)
    expert_out = jnp.dot(activation, wd_vm[0], preferred_element_type=jnp.float32) * expert_gate
    for s in range(shards):
        y_send[s] = expert_out[:, s * cols : (s + 1) * cols].astype(y_send.dtype)
    y_copies = [
        push(y_send.at[peer], y_recv.at[mine], ys_send.at[slot], ys_recv.at[slot], {"kvp": peer})
        for slot, peer in kvp_peers
    ]
    y_recv[mine] = y_send[mine]
    for copy in y_copies:
        copy.wait_recv()
    term = y_recv[0].astype(jnp.float32)
    for s in range(1, shards):
        term = term + y_recv[s].astype(jnp.float32)
    z_all[my_tp] = term.astype(z_all.dtype)
    z_copies = [
        push(z_all.at[my_tp], z_all.at[my_tp], z_send.at[slot], z_recv.at[slot], {"tp": peer})
        for slot, peer in tp_peers
    ]
    for copy in z_copies:
        copy.wait_recv()
    moe = z_all[0].astype(jnp.float32)
    for s in range(1, tps):
        moe = moe + z_all[s].astype(jnp.float32)
    mix_ref[...] = (hidden.astype(jnp.float32) + moe).astype(jnp.bfloat16)
    for copy in sent:
        copy.wait_send()


def on_device_fused(
    queries, keys, values, lengths, out_weight, residual, norm_gain, expert_ids, gate_probs, w_gate, w_up, w_down
):
    shards = lax.axis_size("kvp")
    tps = lax.axis_size("tp")
    batch, width = queries.shape
    heads = width // HEAD
    ctx, lanes = keys.shape[1:]
    cols = residual.shape[1]
    vmem = pl.BlockSpec(memory_space=pltpu.VMEM)
    anywhere = pl.BlockSpec(memory_space=pl.ANY)
    f32, b16 = jnp.float32, jnp.bfloat16

    def sems(count):
        return pltpu.SemaphoreType.DMA((max(count, 1),))

    k, t = shards - 1, tps - 1
    return tuple(pl.pallas_call(
        fused,
        out_shape=(
            pltpu.VMEM((batch, width), f32),
            pltpu.VMEM((batch, cols), b16),
        ),
        in_specs=[anywhere] * 12,
        out_specs=(vmem, vmem),
        scratch_shapes=[
            pltpu.VMEM(queries.shape, b16),
            pltpu.VMEM(keys.shape, b16),
            pltpu.VMEM(values.shape, b16),
            pltpu.SMEM(lengths.shape, jnp.int32),
            pltpu.VMEM(out_weight.shape, b16),
            pltpu.VMEM(residual.shape, b16),
            pltpu.VMEM(norm_gain.shape, b16),
            pltpu.VMEM(expert_ids.shape[::-1], jnp.int32),
            pltpu.VMEM(gate_probs.shape[::-1], f32),
            pltpu.VMEM(w_gate.shape, b16),
            pltpu.VMEM(w_up.shape, b16),
            pltpu.VMEM(w_down.shape, b16),
            pltpu.VMEM((batch * heads, lanes), f32),
            pltpu.VMEM((batch * heads, ctx), f32),
            pltpu.VMEM((batch * heads, lanes), f32),
            pltpu.VMEM((batch * heads, lanes), f32),
            pltpu.VMEM((shards, batch, width), b16),
            pltpu.VMEM((shards, batch // 2, lanes), f32),
            pltpu.VMEM((shards, 1, cols), f32),
            pltpu.VMEM((tps, batch, cols), f32),
            pltpu.VMEM((shards, batch, cols), b16),
            pltpu.VMEM((shards, batch, cols), b16),
            pltpu.VMEM((shards, batch, cols), b16),
            pltpu.VMEM((tps, batch, cols), f32),
            sems(12), sems(k), sems(k), sems(k), sems(k), sems(k), sems(k),
            sems(t), sems(t), sems(k), sems(k), sems(k), sems(k), sems(t), sems(t),
        ],
        compiler_params=pltpu.CompilerParams(
            collective_id=0, has_side_effects=True, vmem_limit_bytes=60 * 1024 * 1024
        ),
    )(
        queries, keys, values, lengths, out_weight, residual, norm_gain,
        expert_ids.T, gate_probs.T, w_gate, w_up, w_down,
    ))


def body(queries, keys, values, lengths, out_weight, residual, norm_gain, expert_ids, gate_probs, w_gate, w_up, w_down):
    args = (queries, keys, values, lengths, out_weight, residual, norm_gain, expert_ids, gate_probs, w_gate, w_up, w_down)
    fits = (
        keys.shape[1] == 128
        and keys.shape[2] == 2 * HEAD
        and w_gate.shape[0] == 1
        and residual.shape[1] % 128 == 0
        and queries.shape[0] == 16
        and queries.shape[1] // HEAD == 16
    )
    return on_device_fused(*args) if fits else on_device(*args)


def solution(mesh):
    return jax.shard_map(
        body,
        mesh=mesh,
        in_specs=(
            P("grp", "tp"),
            P("grp", "kvp", "tp"),
            P("grp", "kvp", "tp"),
            P("grp"),
            P("tp", "kvp"),
            P("grp", "kvp"),
            P("kvp"),
            P("grp", None),
            P("grp", None),
            P("kvp", None, "tp"),
            P("kvp", None, "tp"),
            P("kvp", "tp", None),
        ),
        out_specs=(P("grp", "tp"), P("grp", "kvp")),
        check_vma=False,
    )
```
